512 devices in a mesh: row: 32 (over x, z), col: 16 (over y, core).
Axes of the slice: x: 4, y: 8, z: 8, core: 2. Of those that a mesh axis runs over, the one named last changes fastest.
Arguments:
- matrix: float32 [16384, 16384], P('row', 'col'), as said below
- panel: float32 [16384, 64], P('row'), as said below
Outputs:
- updated: float32 [16384, 16384], P('row', 'col')
- weights: float32 [16384, 64], P('row')
Inputs may be any that keep to these rules, and one draw needn't show every extreme that they name: matrix is exactly symmetric. panel has full column rank.
All inputs are finite; a program needn't handle non-finite values.
Results may differ from the reference program's by a relative error of at most 0.000071.
Values sent between devices are 32-bit elements; how exact they have to be, the bound alone decides.
A program may use at most 64 MiB of HBM per device.

```python
import math
import jax
import jax.numpy as jnp
from jax import lax

N = 16384
B = 64


def draw_matrix(key, part):
    key = jax.random.fold_in(key, 11)
    first = jax.random.fold_in(key, 0)
    base = jax.random.normal(first, (N, N), jnp.float32)
    return (base + base.T) * 0.70710678


def draw_panel(key, part):
    key = jax.random.fold_in(key, 23)
    first, second, third = jax.random.split(key, 3)
    column_scale = jnp.exp(jax.random.uniform(third, (1, B), jnp.float32) * math.log(10.0))
    base = jax.random.normal(first, (N, B), jnp.float32)
    row_scale = jnp.exp(jax.random.uniform(second, (N, 1), jnp.float32) * math.log(10.0))
    return base * row_scale * column_scale


def setup_inputs(seed: int = 0) -> dict:
    key_of = jax.random.split(jax.random.key(seed), 3)
    return {
        "matrix": draw_matrix(jax.random.fold_in(key_of[2], 71), 0),
        "panel": draw_panel(jax.random.fold_in(key_of[2], 71), 0),
    }


def mul(left, right):
    return jnp.dot(left.astype(jnp.float32), right.astype(jnp.float32), precision=lax.Precision.HIGHEST, preferred_element_type=jnp.float32)

def reference(matrix, panel):
    gram = mul(panel.T, panel)
    lower = jnp.linalg.cholesky(gram)
    basis = lax.linalg.triangular_solve(lower, panel.T, left_side=True, lower=True).T
    product = mul(matrix, basis)
    coupling = mul(basis.T, product)
    weights = 2.0 * product - 2.0 * mul(basis, coupling)
    updated = matrix - mul(basis, weights.T) - mul(weights, basis.T)
    return (updated, weights)
```

```python
import jax
import jax.numpy as jnp
from jax import lax
from jax.experimental import pallas as pl
from jax.experimental.pallas import tpu as pltpu
from jax.sharding import PartitionSpec as P

MESH = pl.DeviceIdType.MESH
F32 = jnp.float32
BF16 = jnp.bfloat16
NX, NZ, NC = 4, 8, 16
NR = NX * NZ
B = 64
RL, CL = 512, 1024
TINY = 1e-30
G_RS, G_AG, P_PL, P_Y, Z_RS, Y_AG, Y_A, Y_B, S_Y, S_AG = range(10)


def dot(a, b, dims=((1,), (0,))):
    return lax.dot_general(a, b, (dims, ((), ())), precision=lax.Precision.HIGHEST, preferred_element_type=F32)


def split(x):
    high = x.astype(BF16)
    return high, (x - high.astype(F32)).astype(BF16)


def factors(matrix_hbm, panel_hbm, fr_ref, fc_ref, w_ref,
            a_v, p_v, pt, zt, zsend, zrecv, gsend, grecv, gown, gall,
            pown, pplane, pcols, ypiece, yrow2, yall, yline, yrows, srow, stotal, sline, sall,
            ct, yct, yrt, in_sem, send_sem, recv_sem):
    r = lax.axis_index("row")
    c = lax.axis_index("col")
    x, z = r // NZ, r % NZ

    load_p = pltpu.make_async_copy(panel_hbm, p_v, in_sem.at[0])
    load_a = pltpu.make_async_copy(matrix_hbm, a_v, in_sem.at[1])
    load_p.start()
    load_a.start()

    def plane(i):
        return lax.rem(x + i // NZ, NX) * NZ + lax.rem(z + lax.rem(i, NZ), NZ)

    def line(i):
        return lax.rem(c + i, NC)

    barrier = pltpu.get_barrier_semaphore()

    def greet_plane(i, carry):
        pl.semaphore_signal(barrier, inc=1, device_id=(plane(i), c), device_id_type=MESH)
        return carry

    def greet_line(i, carry):
        pl.semaphore_signal(barrier, inc=1, device_id=(r, line(i)), device_id_type=MESH)
        return carry

    lax.fori_loop(1, NR, greet_plane, 0)
    lax.fori_loop(1, NC, greet_line, 0)

    def to_plane(stage, src, dst):
        def send(i, carry):
            other = plane(i)
            pltpu.make_async_remote_copy(
                src(other), dst, send_sem.at[stage], recv_sem.at[stage],
                device_id=(other, c), device_id_type=MESH).start()
            return carry
        lax.fori_loop(1, NR, send, 0)

    def to_line(stage, src, dst):
        def send(i, carry):
            other = line(i)
            pltpu.make_async_remote_copy(
                src(other), dst, send_sem.at[stage], recv_sem.at[stage],
                device_id=(r, other), device_id_type=MESH).start()
            return carry
        lax.fori_loop(1, NC, send, 0)

    def arrived(stage, buf, n):
        part = buf.at[pl.ds(0, n)]
        pltpu.make_async_copy(part, part, recv_sem.at[stage]).wait()

    def left(stage, buf, n):
        part = buf.at[pl.ds(0, n)]
        pltpu.make_async_copy(part, part, send_sem.at[stage]).wait()

    load_p.wait()
    pt[...] = p_v[...].T
    own_scale = jnp.maximum(jnp.max(jnp.abs(pt[...]), axis=1, keepdims=True), TINY)
    gram = dot(pt[...], pt[...], ((1,), (1,)))
    scale_wide = jnp.broadcast_to(own_scale, (B, 128))
    gsend[:, 0, :] = jnp.concatenate([gram[:32], gram[32:]], axis=1)
    gsend[:, 1, :] = scale_wide[:32]
    gsend[:, 2, :] = scale_wide[32:]
    gsend[:, 3, :] = scale_wide[32:]
    for q in range(4):
        for g in range(4):
            pown[:, q * 4 + g, :] = pt[pl.ds(16 * q, 16), pl.ds(128 * g, 128)]

    pscaled = pt[...] * (1.0 / (128.0 * own_scale))
    load_a.wait()
    zt[...] = dot(pscaled, a_v[...])
    for h in range(2):
        for p in range(2):
            for g in range(4):
                zsend[:, h * 8 + p * 4 + g, :] = zt[pl.ds(32 * p, 32), pl.ds(512 * h + 128 * g, 128)]

    pl.semaphore_wait(barrier, NR - 1 + NC - 1)

    to_plane(G_RS, lambda o: gsend.at[o], grecv.at[r])
    to_plane(Z_RS, lambda o: zsend.at[o], zrecv.at[r])
    to_plane(P_PL, lambda o: pown.at[c], pplane.at[r])
    grecv[r] = gsend[r]
    zrecv[r] = zsend[r]
    pplane[r] = pown[c]

    arrived(G_RS, grecv, NR - 1)
    gown[0, :] = jnp.sum(grecv[:, 0, :], axis=0)
    top = jnp.max(grecv[:, 1:3, :], axis=0)
    gown[1:3, :] = top
    gown[3, :] = top[1]
    to_plane(G_AG, lambda o: gown, gall.at[r])
    gall[r] = gown[...]

    arrived(P_PL, pplane, NR - 1)
    to_line(P_Y, lambda o: pplane.at[pl.ds(2 * o, 2)], pcols.at[c])
    pcols[c] = pplane[pl.ds(2 * c, 2)]

    arrived(Z_RS, zrecv, NR - 1)
    share = grecv[:, 1:3, :] / top[None]
    for h in range(2):
        for p in range(2):
            rows = pl.ds(h * 8 + p * 4, 4)
            ypiece[rows, :] = jnp.sum(zrecv[:, rows, :] * share[:, p:p + 1, :], axis=0)
    to_plane(Y_AG, lambda o: ypiece, yall.at[r])
    to_line(Y_A, lambda o: ypiece, yline.at[c])
    yall[r] = ypiece[...]
    yline[c] = ypiece[...]
    yrow2[...] = jnp.zeros_like(yrow2)
    for h in range(2):
        for p in range(2):
            for g in range(4):
                yrow2[pl.ds(p, 1), pl.ds(512 * h + 128 * g, 128)] = ypiece[pl.ds(h * 8 + p * 4 + g, 1), :]

    arrived(G_AG, gall, NR - 1)
    scale = jnp.concatenate([gall[:, 1, :], gall[:, 2, :]], axis=0) * 128.0
    inv_scale = 1.0 / scale

    arrived(P_Y, pcols, NC - 1)
    for h in range(2):
        for q in range(4):
            for g in range(4):
                block = pcols[:, h, q * 4 + g, :]
                ct[pl.ds(16 * q, 16), pl.ds(512 * h + 128 * g, 128)] = block * inv_scale[16 * q:16 * q + 16]
    part = dot(yrow2[...], ct[...], ((1,), (1,)))
    srow[...] = jnp.concatenate([part[0:1], part[1:2]], axis=1)
    to_line(S_Y, lambda o: srow, sline.at[c])
    sline[c] = srow[...]

    arrived(Y_A, yline, NC - 1)

    def send_rows(i, carry):
        other = plane(i)
        pltpu.make_async_remote_copy(
            yline.at[other // 2, pl.ds(pl.multiple_of(lax.rem(other, 2) * 8, 8), 8)], yrows.at[r],
            send_sem.at[Y_B], recv_sem.at[Y_B],
            device_id=(other, c), device_id_type=MESH).start()
        return carry
    lax.fori_loop(1, NR, send_rows, 0)
    yrows[r] = yline[r // 2, pl.ds(pl.multiple_of(lax.rem(r, 2) * 8, 8), 8), :]

    g32 = gall[:, 0, :]
    gram = jnp.concatenate([g32[:, :B], g32[:, B:]], axis=0)
    inv64 = inv_scale[:, :B]
    gram = gram * inv64 * inv64.T
    row_id = lax.broadcasted_iota(jnp.int32, (B, 2 * B), 0)
    lane_id = lax.broadcasted_iota(jnp.int32, (B, 2 * B), 1)
    work = jnp.concatenate([gram, jnp.where(row_id == lane_id, 1.0, 0.0)[:, :B]], axis=1)
    for j in range(B - 1):
        ratio = work[:, j:j + 1] * (1.0 / work[j:j + 1, j:j + 1])
        work = work - jnp.where(row_id > j, ratio, 0.0) * work[j:j + 1, :]
    pivots = jnp.sum(jnp.where(row_id == lane_id, work, 0.0), axis=1, keepdims=True)
    root = lax.rsqrt(pivots)
    root = root * (1.5 - 0.5 * pivots * root * root)
    inv_lower = work[:, B:] * root

    arrived(S_Y, sline, NC - 1)
    stotal[...] = jnp.sum(sline[...], axis=0)
    to_plane(S_AG, lambda o: stotal, sall.at[r])
    sall[r] = stotal[...]

    basis_r = dot(inv_lower, pt[...] * inv_scale[:, :1])
    basis_c = dot(inv_lower, ct[...])

    arrived(Y_AG, yall, NR - 1)
    for h in range(2):
        for p in range(2):
            for g in range(4):
                yct[pl.ds(32 * p, 32), pl.ds(512 * h + 128 * g, 128)] = yall[:, h * 8 + p * 4 + g, :]
    product_c = dot(inv_lower, yct[...])
    arrived(Y_B, yrows, NR - 1)
    for p in range(2):
        for g in range(4):
            yrt[pl.ds(32 * p, 32), pl.ds(128 * g, 128)] = yrows[:, p * 4 + g, :]
    product_r = dot(inv_lower, yrt[...])

    arrived(S_AG, sall, NR - 1)
    s32 = sall[:, 0, :]
    inner = jnp.concatenate([s32[:, :B], s32[:, B:]], axis=0)
    coupling = dot(dot(inv_lower, inner), inv_lower, ((1,), (1,)))
    weights_r = 2.0 * product_r - 2.0 * dot(coupling, basis_r)
    weights_c = 2.0 * product_c - 2.0 * dot(coupling, basis_c)

    left_t = jnp.concatenate([basis_r, weights_r], axis=0).T
    w_ref[...] = left_t[:, B:]
    high, low = split(left_t)
    fr_ref[:, 0:128] = high
    fr_ref[:, 128:256] = low
    fr_ref[:, 256:384] = high
    high, low = split(jnp.concatenate([weights_c, basis_c], axis=0))
    fc_ref[0:128, :] = high
    fc_ref[128:256, :] = high
    fc_ref[256:384, :] = low

    left(G_RS, gsend, NR - 1)
    left(G_AG, gall, NR - 1)
    left(P_PL, pplane, NR - 1)
    left(P_Y, pcols, NC - 1)
    left(Z_RS, zsend, NR - 1)
    left(Y_AG, yall, NR - 1)
    left(Y_A, yline, NC - 1)
    left(Y_B, yrows, NR - 1)
    left(S_Y, sline, NC - 1)
    left(S_AG, sall, NR - 1)


def apply_update(matrix_ref, fr_ref, fc_ref, w_ref, out_ref, w_out):
    out_ref[...] = matrix_ref[...] - jnp.dot(fr_ref[...], fc_ref[...], preferred_element_type=F32)

    @pl.when(pl.program_id(0) == 0)
    def _():
        w_out[...] = w_ref[...]


def local(matrix, panel):
    vmem = pl.BlockSpec(memory_space=pltpu.VMEM)
    anywhere = pl.BlockSpec(memory_space=pl.ANY)
    fr, fc, w = pl.pallas_call(
        factors,
        out_shape=(jax.ShapeDtypeStruct((RL, 384), BF16), jax.ShapeDtypeStruct((384, CL), BF16),
                   jax.ShapeDtypeStruct((RL, B), F32)),
        in_specs=[anywhere, anywhere],
        out_specs=(vmem, vmem, vmem),
        scratch_shapes=[
            pltpu.VMEM((RL, CL), F32), pltpu.VMEM((RL, B), F32), pltpu.VMEM((B, RL), F32),
            pltpu.VMEM((B, CL), F32),
            pltpu.VMEM((NR, 16, 128), F32), pltpu.VMEM((NR, 16, 128), F32),
            pltpu.VMEM((NR, 4, 128), F32), pltpu.VMEM((NR, 4, 128), F32),
            pltpu.VMEM((4, 128), F32), pltpu.VMEM((NR, 4, 128), F32),
            pltpu.VMEM((NC, 16, 128), F32), pltpu.VMEM((NR, 16, 128), F32), pltpu.VMEM((NC, 2, 16, 128), F32),
            pltpu.VMEM((16, 128), F32), pltpu.VMEM((8, CL), F32), pltpu.VMEM((NR, 16, 128), F32),
            pltpu.VMEM((NC, 16, 128), F32), pltpu.VMEM((NR, 8, 128), F32),
            pltpu.VMEM((1, 128), F32), pltpu.VMEM((1, 128), F32),
            pltpu.VMEM((NC, 1, 128), F32), pltpu.VMEM((NR, 1, 128), F32),
            pltpu.VMEM((B, CL), F32), pltpu.VMEM((B, CL), F32), pltpu.VMEM((B, RL), F32),
            pltpu.SemaphoreType.DMA((2,)), pltpu.SemaphoreType.DMA((10,)), pltpu.SemaphoreType.DMA((10,)),
        ],
        compiler_params=pltpu.CompilerParams(
            collective_id=0, has_side_effects=True, vmem_limit_bytes=40 << 20),
        name="factors",
    )(matrix, panel)
    tile = 128
    return pl.pallas_call(
        apply_update,
        grid=(RL // tile,),
        out_shape=(jax.ShapeDtypeStruct((RL, CL), F32), jax.ShapeDtypeStruct((RL, B), F32)),
        in_specs=[pl.BlockSpec((tile, CL), lambda i: (i, 0)), pl.BlockSpec((tile, 384), lambda i: (i, 0)),
                  pl.BlockSpec((384, CL), lambda i: (0, 0)), pl.BlockSpec((RL, B), lambda i: (0, 0))],
        out_specs=(pl.BlockSpec((tile, CL), lambda i: (i, 0)), pl.BlockSpec((RL, B), lambda i: (0, 0))),
        name="apply_update",
    )(matrix, fr, fc, w)


def solution(mesh):
    specs = (P("row", "col"), P("row", None))
    return jax.shard_map(local, mesh=mesh, in_specs=specs, out_specs=specs, check_vma=False)
```

```python
import jax
import jax.numpy as jnp
from jax import lax
from jax.experimental import pallas as pl
from jax.experimental.pallas import tpu as pltpu
from jax.sharding import PartitionSpec as P

MESH = pl.DeviceIdType.MESH
F32 = jnp.float32
BF16 = jnp.bfloat16
NX, NZ, NC = 4, 8, 16
NR = NX * NZ
NG = NX * NC
B = 64
RL, CL = 512, 1024
QL = 256
TINY = 1e-30
G_RS, G_AG, P_SUB, P_ZR, P_XR, Z_RS, Y_AG, Y_B, S_RS, S_AG = range(10)
STAGES = 10


def dot(a, b, dims=((1,), (0,))):
    return lax.dot_general(a, b, (dims, ((), ())), precision=lax.Precision.HIGHEST, preferred_element_type=F32)


def split(x):
    high = x.astype(BF16)
    return high, (x - high.astype(F32)).astype(BF16)


def split3(x):
    high = x.astype(BF16)
    rest = x - high.astype(F32)
    mid = rest.astype(BF16)
    return high, mid, (rest - mid.astype(F32)).astype(BF16)


def dot6(a, b):
    parts = jnp.concatenate(split3(a), axis=0)
    bh, bm, bl = split3(b)
    one = jnp.dot(parts, bh, preferred_element_type=F32)
    two = jnp.dot(parts[:2 * B], bm, preferred_element_type=F32)
    three = jnp.dot(parts[:B], bl, preferred_element_type=F32)
    return one[:B] + ((one[B:2 * B] + two[:B]) + (one[2 * B:] + two[B:] + three))


def dot3(at, b):
    ah, al = split(at.T)
    bh, bl = split(b)
    return jnp.dot(jnp.concatenate([ah, al, ah], axis=1), jnp.concatenate([bh, bh, bl], axis=0),
                   preferred_element_type=F32)


def inverse_factor(gram):
    row_id = lax.broadcasted_iota(jnp.int32, (B, 2 * B), 0)
    lane_id = lax.broadcasted_iota(jnp.int32, (B, 2 * B), 1)
    work = jnp.concatenate([gram, jnp.where(row_id == lane_id, 1.0, 0.0)[:, :B]], axis=1)
    step = 8
    for j in range(0, B, step):
        cols = [jnp.broadcast_to(work[:, j + t:j + t + 1], (B, 2 * B)) for t in range(step)]
        rows = [work[j + t:j + t + 1, :] for t in range(step)]
        for t in range(step):
            at = j + t
            ratio = jnp.where(row_id > at, cols[t] * (1.0 / cols[t][at:at + 1, :]), 0.0)
            work = work - ratio * rows[t]
            for u in range(t + 1, step):
                cols[u] = cols[u] - ratio * cols[t][j + u:j + u + 1, :]
                rows[u] = rows[u] - ratio[j + u:j + u + 1, :] * rows[t]
    pivots = jnp.sum(jnp.where(row_id == lane_id, work, 0.0), axis=1, keepdims=True)
    root = lax.rsqrt(pivots)
    root = root * (1.5 - 0.5 * pivots * root * root)
    return work[:, B:] * root


def panel_step(matrix_hbm, panel_hbm, out_ref, w_ref,
               pt, zt, zrecv, gsend, grecv, gown, gall, ct, spart,
               ypiece, yct, yrt, ssend, srecv, sown, sall, in_sem, send_sem, recv_sem):
    r = lax.axis_index("row")
    c = lax.axis_index("col")
    x, z = r // NZ, r % NZ
    feats = pl.ds(pl.multiple_of(z * 8, 8), 8)
    quarter = pl.ds(pl.multiple_of(x * QL, QL), QL)
    half = pl.ds(pl.multiple_of(lax.rem(x, 2) * QL, QL), QL)

    load_p = pltpu.make_async_copy(panel_hbm, pt, in_sem.at[0])
    load_a = pltpu.make_async_copy(matrix_hbm, out_ref, in_sem.at[1])
    load_p.start()
    load_a.start()

    def plane(i):
        return lax.rem(x + i // NZ, NX) * NZ + lax.rem(z + lax.rem(i, NZ), NZ)

    def line(i):
        return lax.rem(c + i, NC)

    barrier = pltpu.get_barrier_semaphore()

    def greet_plane(i, carry):
        pl.semaphore_signal(barrier, inc=1, device_id=(plane(i), c), device_id_type=MESH)
        return carry

    def greet_line(i, carry):
        pl.semaphore_signal(barrier, inc=1, device_id=(r, line(i)), device_id_type=MESH)
        return carry

    lax.fori_loop(1, NR, greet_plane, 0)
    lax.fori_loop(1, NC, greet_line, 0)

    def push(stage, src, dst, row, col):
        pltpu.make_async_remote_copy(
            src, dst, send_sem.at[stage], recv_sem.at[stage],
            device_id=(row, col), device_id_type=MESH).start()

    def to_plane(stage, src, dst):
        def send(i, carry):
            other = plane(i)
            push(stage, src(other), dst, other, c)
            return carry
        lax.fori_loop(1, NR, send, 0)

    def to_line(stage, src, dst):
        def send(i, carry):
            other = line(i)
            push(stage, src(other), dst, r, other)
            return carry
        lax.fori_loop(1, NC, send, 0)

    def arrived(stage, part):
        pltpu.make_async_copy(part, part, recv_sem.at[stage]).wait()

    def left(stage, part):
        pltpu.make_async_copy(part, part, send_sem.at[stage]).wait()

    def first(buf, n):
        return buf.at[pl.ds(0, n)]

    load_p.wait()
    own_scale = jnp.maximum(jnp.max(jnp.abs(pt[...]), axis=1, keepdims=True), TINY)
    gram = dot(pt[...], pt[...], ((1,), (1,)))
    gsend[:, 0, :] = jnp.concatenate([gram[:32], gram[32:]], axis=1)
    scale_row = jnp.broadcast_to(own_scale, (B, 128)).T[0:1, :]
    gsend[:, 1, :] = jnp.broadcast_to(jnp.concatenate([scale_row, scale_row], axis=1), (NR, 128))

    def multiply():
        load_a.wait()
        zt[...] = dot6(pt[...] * (1.0 / (128.0 * own_scale)), out_ref[...])

    @pl.when(z < NZ // 2)
    def _():
        multiply()

    pl.semaphore_wait(barrier, NR - 1 + NC - 1)
    def spread_quarters(i, carry):
        ox = 2 * lax.rem(r, 2) + i // NZ
        oz = lax.rem(z + lax.rem(i, NZ), NZ)
        other = ox * NZ + oz

        @pl.when(other != r)
        def _():
            push(P_SUB, pt.at[pl.ds(pl.multiple_of(oz * 8, 8), 8), pl.ds(pl.multiple_of((i // NZ) * QL, QL), QL)],
                 ct.at[pl.ds(pl.multiple_of(oz * 8, 8), 8), pl.ds(pl.multiple_of(ox * QL, QL), QL)], other, c)
        return carry

    @pl.when(c == r // 2)
    def _():
        lax.fori_loop(0, 2 * NZ, spread_quarters, 0)

    own_quarter = r == 2 * c + x // 2

    @pl.when(own_quarter)
    def _():
        ct[feats, quarter] = pt[feats, half]

    to_plane(G_RS, lambda o: gsend.at[o], grecv.at[r])
    grecv[r] = gsend[r]

    @pl.when(z >= NZ // 2)
    def _():
        multiply()

    def send_pieces(i, carry):
        other = plane(i)
        push(Z_RS, zt.at[pl.ds(pl.multiple_of(lax.rem(other, NZ) * 8, 8), 8),
                         pl.ds(pl.multiple_of((other // NZ) * QL, QL), QL)], zrecv.at[r], other, c)
        return carry
    lax.fori_loop(1, NR, send_pieces, 0)
    zrecv[r] = zt[feats, quarter]

    @pl.when(jnp.logical_not(own_quarter))
    def _():
        arrived(P_SUB, ct.at[feats, quarter])

    def hand_round(i, carry):
        push(P_ZR, ct.at[feats, quarter], ct.at[feats, quarter], x * NZ + lax.rem(z + i, NZ), c)
        return carry
    lax.fori_loop(1, NZ, hand_round, 0)

    arrived(G_RS, first(grecv, NR - 1))
    gown[...] = jnp.sum(grecv[:, 0, :], axis=0, keepdims=True)
    to_plane(G_AG, lambda o: gown, gall.at[r])
    gall[r] = gown[...]
    scales = jnp.broadcast_to(grecv[:, 1, :][None], (4, NR, 128)).reshape(4 * NR, 128).T[:B]
    scale = jnp.max(scales, axis=1, keepdims=True)
    inv_scale = 1.0 / (128.0 * scale)
    spart[...] = scales * (1.0 / scale)
    share = spart[feats, :]

    arrived(P_ZR, first(zrecv, NZ - 1))
    arrived(Z_RS, first(zrecv, NR - 1))
    total = zrecv[0] * share[:, 0:1]
    for k in range(1, NR):
        total = total + zrecv[k] * share[:, k:k + 1]
    ypiece[...] = total
    part = dot(total, ct[:, quarter] * inv_scale, ((1,), (1,)))
    ssend[...] = jnp.concatenate([part[:4], part[4:]], axis=1)

    def send_coupling(i, carry):
        push(S_RS, ssend, srecv.at[x * NC + c],
             lax.rem(x + i // NC, NX) * NZ + z, lax.rem(c + lax.rem(i, NC), NC))
        return carry
    lax.fori_loop(1, NG, send_coupling, 0)
    srecv[x * NC + c] = ssend[...]

    def send_rows(i, carry):
        block = 2 * c + x // 2
        other = line(i)

        @pl.when(jnp.logical_or(block != r, other != c))
        def _():
            push(Y_B, ypiece, yrt.at[feats, half], block, other)
        return carry
    lax.fori_loop(0, NC, send_rows, 0)

    @pl.when(own_quarter)
    def _():
        yrt[feats, half] = total
    to_plane(Y_AG, lambda o: ypiece, yct.at[feats, quarter])
    yct[feats, quarter] = total

    def hand_across(i, carry):
        push(P_XR, ct.at[:, quarter], ct.at[:, quarter], lax.rem(x + i, NX) * NZ + z, c)
        return carry
    lax.fori_loop(1, NX, hand_across, 0)

    arrived(G_AG, first(gall, NR - 1))
    g32 = gall[:, 0, :]
    gram = jnp.concatenate([g32[:, :B], g32[:, B:]], axis=0)
    inv_row = jnp.broadcast_to(inv_scale, (B, 128)).T[0:1, :]
    inv_lower = inverse_factor(gram * inv_scale * inv_row)
    unscaled = inv_lower * inv_row
    basis_r = dot(unscaled, pt[...])

    arrived(S_RS, first(srecv, NG - 1))
    sown[...] = jnp.sum(srecv[...], axis=0)

    def send_rows_of_coupling(i, carry):
        push(S_AG, sown, sall.at[z], x * NZ + lax.rem(z + i, NZ), c)
        return carry
    lax.fori_loop(1, NZ, send_rows_of_coupling, 0)
    sall[z] = sown[...]

    arrived(Y_AG, first(zrecv, NR - 1))
    product_c = dot(inv_lower, yct[...])

    arrived(P_XR, ct.at[:, pl.ds(0, (NX - 1) * QL)])
    basis_c = dot(unscaled, ct[...])

    @pl.when(own_quarter)
    def _():
        arrived(Y_B, first(zrecv, 15))

    @pl.when(jnp.logical_not(own_quarter))
    def _():
        arrived(Y_B, first(zrecv, 16))
    product_r = dot(inv_lower, yrt[...])

    tile = 128
    for t in range(RL // tile):
        cols = pl.ds(t * tile, tile)
        ours = jnp.concatenate([basis_r[:, t * tile:(t + 1) * tile], product_r[:, t * tile:(t + 1) * tile]], axis=0)
        out_ref[cols, :] -= dot3(2.0 * ours, jnp.concatenate([product_c, basis_c], axis=0))

    arrived(S_AG, first(sall, NZ - 1))
    inner = jnp.concatenate([sall[k][:, h * B:(h + 1) * B] for k in range(NZ) for h in range(2)], axis=0)
    coupling = dot(dot(inv_lower, inner), inv_lower, ((1,), (1,)))
    w_ref[...] = 2.0 * product_r - 2.0 * dot(coupling, basis_r)
    turned = 4.0 * dot(coupling, basis_c)
    for t in range(RL // tile):
        cols = pl.ds(t * tile, tile)
        out_ref[cols, :] += dot3(basis_r[:, t * tile:(t + 1) * tile], turned)

    left(G_RS, first(gsend, NR - 1))
    left(G_AG, first(gall, NR - 1))
    left(Z_RS, first(zrecv, NR - 1))
    left(P_XR, ct.at[:, pl.ds(0, (NX - 1) * QL)])
    left(Y_AG, first(zrecv, NR - 1))
    left(P_ZR, first(zrecv, NZ - 1))
    left(S_RS, first(srecv, NG - 1))
    left(S_AG, first(sall, NZ - 1))

    @pl.when(own_quarter)
    def _():
        left(Y_B, first(zrecv, 15))

    @pl.when(jnp.logical_not(own_quarter))
    def _():
        left(Y_B, first(zrecv, 16))

    @pl.when(own_quarter)
    def _():
        left(P_SUB, first(zrecv, 15))

    @pl.when(jnp.logical_and(c == r // 2, jnp.logical_not(own_quarter)))
    def _():
        left(P_SUB, first(zrecv, 16))


def local(matrix, panel):
    vmem = pl.BlockSpec(memory_space=pltpu.VMEM)
    in_hbm = pl.BlockSpec(memory_space=pltpu.HBM)
    updated, weights = pl.pallas_call(
        panel_step,
        out_shape=(jax.ShapeDtypeStruct((RL, CL), F32), jax.ShapeDtypeStruct((B, RL), F32)),
        in_specs=[in_hbm, in_hbm],
        out_specs=(vmem, vmem),
        scratch_shapes=[
            pltpu.VMEM((B, RL), F32),
            pltpu.VMEM((B, CL), F32),
            pltpu.VMEM((NR, 8, QL), F32),
            pltpu.VMEM((NR, 2, 128), F32),
            pltpu.VMEM((NR, 2, 128), F32),
            pltpu.VMEM((1, 128), F32),
            pltpu.VMEM((NR, 1, 128), F32),
            pltpu.VMEM((B, CL), F32),
            pltpu.VMEM((B, 128), F32),
            pltpu.VMEM((8, QL), F32),
            pltpu.VMEM((B, CL), F32),
            pltpu.VMEM((B, RL), F32),
            pltpu.VMEM((4, 128), F32),
            pltpu.VMEM((NG, 4, 128), F32),
            pltpu.VMEM((4, 128), F32),
            pltpu.VMEM((NZ, 4, 128), F32),
            pltpu.SemaphoreType.DMA((2,)), pltpu.SemaphoreType.DMA((STAGES,)), pltpu.SemaphoreType.DMA((STAGES,)),
        ],
        compiler_params=pltpu.CompilerParams(
            collective_id=0, has_side_effects=True, vmem_limit_bytes=24 << 20),
        name="panel_step",
    )(pltpu.with_memory_space_constraint(matrix, pltpu.HBM), pltpu.with_memory_space_constraint(panel.T, pltpu.HBM))
    return updated, weights.T


def solution(mesh):
    specs = (P("row", "col"), P("row", None))
    return jax.shard_map(local, mesh=mesh, in_specs=specs, out_specs=specs, check_vma=False)
```

```python
import jax
import jax.numpy as jnp
from jax import lax
from jax.experimental import pallas as pl
from jax.experimental.pallas import tpu as pltpu
from jax.sharding import PartitionSpec as P

MESH = pl.DeviceIdType.MESH
F32 = jnp.float32
BF16 = jnp.bfloat16
NX, NZ, NC = 4, 8, 16
NR = NX * NZ
NG = NX * NC
B = 64
RL, CL = 512, 1024
QL = 256
TINY = 1e-30
G_RS, G_AG, P_SUB, P_ZR, P_XR, Z_RS, Y_ZR, Y_XR, Y_B, S_RS, S_AG = range(11)
STAGES = 11


def dot(a, b, dims=((1,), (0,))):
    return lax.dot_general(a, b, (dims, ((), ())), precision=lax.Precision.HIGHEST, preferred_element_type=F32)


def split(x):
    high = x.astype(BF16)
    return high, (x - high.astype(F32)).astype(BF16)


def split3(x):
    high = x.astype(BF16)
    rest = x - high.astype(F32)
    mid = rest.astype(BF16)
    return high, mid, (rest - mid.astype(F32)).astype(BF16)


def dot6(a, b):
    parts = jnp.concatenate(split3(a), axis=0)
    bh, bm, bl = split3(b)
    one = jnp.dot(parts, bh, preferred_element_type=F32)
    two = jnp.dot(parts[:2 * B], bm, preferred_element_type=F32)
    three = jnp.dot(parts[:B], bl, preferred_element_type=F32)
    return one[:B] + ((one[B:2 * B] + two[:B]) + (one[2 * B:] + two[B:] + three))


def dot3(at, b):
    ah, al = split(at.T)
    bh, bl = split(b)
    return jnp.dot(jnp.concatenate([ah, al, ah], axis=1), jnp.concatenate([bh, bh, bl], axis=0),
                   preferred_element_type=F32)


def inverse_factor(gram):
    row_id = lax.broadcasted_iota(jnp.int32, (B, 2 * B), 0)
    lane_id = lax.broadcasted_iota(jnp.int32, (B, 2 * B), 1)
    work = jnp.concatenate([gram, jnp.where(row_id == lane_id, 1.0, 0.0)[:, :B]], axis=1)
    step = 8
    for j in range(0, B, step):
        cols = [jnp.broadcast_to(work[:, j + t:j + t + 1], (B, 2 * B)) for t in range(step)]
        rows = [work[j + t:j + t + 1, :] for t in range(step)]
        for t in range(step):
            at = j + t
            ratio = jnp.where(row_id > at, cols[t] * (1.0 / cols[t][at:at + 1, :]), 0.0)
            work = work - ratio * rows[t]
            for u in range(t + 1, step):
                cols[u] = cols[u] - ratio * cols[t][j + u:j + u + 1, :]
                rows[u] = rows[u] - ratio[j + u:j + u + 1, :] * rows[t]
    pivots = jnp.sum(jnp.where(row_id == lane_id, work, 0.0), axis=1, keepdims=True)
    root = lax.rsqrt(pivots)
    root = root * (1.5 - 0.5 * pivots * root * root)
    return work[:, B:] * root


def panel_step(matrix_hbm, panel_hbm, out_ref, w_ref,
               pt, zt, zrecv, gsend, grecv, gown, gall, ct, spart,
               ypiece, yct, yrt, ssend, srecv, sown, sall, in_sem, send_sem, recv_sem):
    r = lax.axis_index("row")
    c = lax.axis_index("col")
    x, z = r // NZ, r % NZ
    feats = pl.ds(pl.multiple_of(z * 8, 8), 8)
    quarter = pl.ds(pl.multiple_of(x * QL, QL), QL)
    half = pl.ds(pl.multiple_of(lax.rem(x, 2) * QL, QL), QL)

    load_p = pltpu.make_async_copy(panel_hbm, pt, in_sem.at[0])
    load_a = pltpu.make_async_copy(matrix_hbm, out_ref, in_sem.at[1])
    load_p.start()
    load_a.start()

    def plane(i):
        return lax.rem(x + i // NZ, NX) * NZ + lax.rem(z + lax.rem(i, NZ), NZ)

    def line(i):
        return lax.rem(c + i, NC)

    barrier = pltpu.get_barrier_semaphore()

    def greet_plane(i, carry):
        pl.semaphore_signal(barrier, inc=1, device_id=(plane(i), c), device_id_type=MESH)
        return carry

    def greet_line(i, carry):
        pl.semaphore_signal(barrier, inc=1, device_id=(r, line(i)), device_id_type=MESH)
        return carry

    lax.fori_loop(1, NR, greet_plane, 0)
    lax.fori_loop(1, NC, greet_line, 0)

    def push(stage, src, dst, row, col):
        pltpu.make_async_remote_copy(
            src, dst, send_sem.at[stage], recv_sem.at[stage],
            device_id=(row, col), device_id_type=MESH).start()

    def to_plane(stage, src, dst):
        def send(i, carry):
            other = plane(i)
            push(stage, src(other), dst, other, c)
            return carry
        lax.fori_loop(1, NR, send, 0)

    def to_line(stage, src, dst):
        def send(i, carry):
            other = line(i)
            push(stage, src(other), dst, r, other)
            return carry
        lax.fori_loop(1, NC, send, 0)

    def arrived(stage, part):
        pltpu.make_async_copy(part, part, recv_sem.at[stage]).wait()

    def left(stage, part):
        pltpu.make_async_copy(part, part, send_sem.at[stage]).wait()

    def first(buf, n):
        return buf.at[pl.ds(0, n)]

    load_p.wait()
    own_scale = jnp.maximum(jnp.max(jnp.abs(pt[...]), axis=1, keepdims=True), TINY)
    gram = dot(pt[...], pt[...], ((1,), (1,)))
    gsend[:, 0, :] = jnp.concatenate([gram[:32], gram[32:]], axis=1)
    scale_row = jnp.broadcast_to(own_scale, (B, 128)).T[0:1, :]
    gsend[:, 1, :] = jnp.broadcast_to(jnp.concatenate([scale_row, scale_row], axis=1), (NR, 128))

    def multiply():
        load_a.wait()
        zt[...] = dot6(pt[...] * (1.0 / (128.0 * own_scale)), out_ref[...])

    @pl.when(z < NZ // 2)
    def _():
        multiply()

    pl.semaphore_wait(barrier, NR - 1 + NC - 1)
    def spread_quarters(i, carry):
        ox = 2 * lax.rem(r, 2) + i // NZ
        oz = lax.rem(z + lax.rem(i, NZ), NZ)
        other = ox * NZ + oz

        @pl.when(other != r)
        def _():
            push(P_SUB, pt.at[pl.ds(pl.multiple_of(oz * 8, 8), 8), pl.ds(pl.multiple_of((i // NZ) * QL, QL), QL)],
                 ct.at[pl.ds(pl.multiple_of(oz * 8, 8), 8), pl.ds(pl.multiple_of(ox * QL, QL), QL)], other, c)
        return carry

    @pl.when(c == r // 2)
    def _():
        lax.fori_loop(0, 2 * NZ, spread_quarters, 0)

    own_quarter = r == 2 * c + x // 2

    @pl.when(own_quarter)
    def _():
        ct[feats, quarter] = pt[feats, half]

    to_plane(G_RS, lambda o: gsend.at[o], grecv.at[r])
    grecv[r] = gsend[r]

    @pl.when(z >= NZ // 2)
    def _():
        multiply()

    def send_pieces(i, carry):
        other = plane(i)
        push(Z_RS, zt.at[pl.ds(pl.multiple_of(lax.rem(other, NZ) * 8, 8), 8),
                         pl.ds(pl.multiple_of((other // NZ) * QL, QL), QL)], zrecv.at[r], other, c)
        return carry
    lax.fori_loop(1, NR, send_pieces, 0)
    zrecv[r] = zt[feats, quarter]

    @pl.when(jnp.logical_not(own_quarter))
    def _():
        arrived(P_SUB, ct.at[feats, quarter])

    def hand_round(i, carry):
        push(P_ZR, ct.at[feats, quarter], ct.at[feats, quarter], x * NZ + lax.rem(z + i, NZ), c)
        return carry
    lax.fori_loop(1, NZ, hand_round, 0)

    arrived(G_RS, first(grecv, NR - 1))
    gown[...] = jnp.sum(grecv[:, 0, :], axis=0, keepdims=True)
    to_plane(G_AG, lambda o: gown, gall.at[r])
    gall[r] = gown[...]
    scales = jnp.broadcast_to(grecv[:, 1, :][None], (4, NR, 128)).reshape(4 * NR, 128).T[:B]
    scale = jnp.max(scales, axis=1, keepdims=True)
    inv_scale = 1.0 / (128.0 * scale)
    spart[...] = scales * (1.0 / scale)
    share = spart[feats, :]

    arrived(P_ZR, first(zrecv, NZ - 1))
    arrived(Z_RS, first(zrecv, NR - 1))
    total = zrecv[0] * share[:, 0:1]
    for k in range(1, NR):
        total = total + zrecv[k] * share[:, k:k + 1]
    ypiece[...] = total
    part = dot(total, ct[:, quarter] * inv_scale, ((1,), (1,)))
    ssend[...] = jnp.concatenate([part[:4], part[4:]], axis=1)

    def send_coupling(i, carry):
        push(S_RS, ssend, srecv.at[x * NC + c],
             lax.rem(x + i // NC, NX) * NZ + z, lax.rem(c + lax.rem(i, NC), NC))
        return carry
    lax.fori_loop(1, NG, send_coupling, 0)
    srecv[x * NC + c] = ssend[...]

    def send_rows(i, carry):
        block = 2 * c + x // 2
        other = line(i)

        @pl.when(jnp.logical_or(block != r, other != c))
        def _():
            push(Y_B, ypiece, yrt.at[feats, half], block, other)
        return carry
    lax.fori_loop(0, NC, send_rows, 0)

    @pl.when(own_quarter)
    def _():
        yrt[feats, half] = total

    def hand_product(i, carry):
        push(Y_ZR, ypiece, yct.at[feats, quarter], x * NZ + lax.rem(z + i, NZ), c)
        return carry
    lax.fori_loop(1, NZ, hand_product, 0)
    yct[feats, quarter] = total

    def hand_across(i, carry):
        push(P_XR, ct.at[:, quarter], ct.at[:, quarter], lax.rem(x + i, NX) * NZ + z, c)
        return carry
    lax.fori_loop(1, NX, hand_across, 0)

    arrived(G_AG, first(gall, NR - 1))
    g32 = gall[:, 0, :]
    gram = jnp.concatenate([g32[:, :B], g32[:, B:]], axis=0)
    inv_row = jnp.broadcast_to(inv_scale, (B, 128)).T[0:1, :]
    inv_lower = inverse_factor(gram * inv_scale * inv_row)
    unscaled = inv_lower * inv_row
    arrived(Y_ZR, first(zrecv, NZ - 1))

    def hand_product_across(i, carry):
        push(Y_XR, yct.at[:, quarter], yct.at[:, quarter], lax.rem(x + i, NX) * NZ + z, c)
        return carry
    lax.fori_loop(1, NX, hand_product_across, 0)

    basis_r = dot(unscaled, pt[...])

    arrived(S_RS, first(srecv, NG - 1))
    sown[...] = jnp.sum(srecv[...], axis=0)

    def send_rows_of_coupling(i, carry):
        push(S_AG, sown, sall.at[z], x * NZ + lax.rem(z + i, NZ), c)
        return carry
    lax.fori_loop(1, NZ, send_rows_of_coupling, 0)
    sall[z] = sown[...]

    arrived(Y_XR, yct.at[:, pl.ds(0, (NX - 1) * QL)])
    product_c = dot(inv_lower, yct[...])

    arrived(P_XR, ct.at[:, pl.ds(0, (NX - 1) * QL)])
    basis_c = dot(unscaled, ct[...])

    @pl.when(own_quarter)
    def _():
        arrived(Y_B, first(zrecv, 15))

    @pl.when(jnp.logical_not(own_quarter))
    def _():
        arrived(Y_B, first(zrecv, 16))
    product_r = dot(inv_lower, yrt[...])

    tile = 128
    for t in range(RL // tile):
        cols = pl.ds(t * tile, tile)
        ours = jnp.concatenate([basis_r[:, t * tile:(t + 1) * tile], product_r[:, t * tile:(t + 1) * tile]], axis=0)
        out_ref[cols, :] -= dot3(2.0 * ours, jnp.concatenate([product_c, basis_c], axis=0))

    arrived(S_AG, first(sall, NZ - 1))
    inner = jnp.concatenate([sall[k][:, h * B:(h + 1) * B] for k in range(NZ) for h in range(2)], axis=0)
    coupling = dot(dot(inv_lower, inner), inv_lower, ((1,), (1,)))
    w_ref[...] = 2.0 * product_r - 2.0 * dot(coupling, basis_r)
    turned = 4.0 * dot(coupling, basis_c)
    for t in range(RL // tile):
        cols = pl.ds(t * tile, tile)
        out_ref[cols, :] += dot3(basis_r[:, t * tile:(t + 1) * tile], turned)

    left(G_RS, first(gsend, NR - 1))
    left(G_AG, first(gall, NR - 1))
    left(Z_RS, first(zrecv, NR - 1))
    left(P_XR, ct.at[:, pl.ds(0, (NX - 1) * QL)])
    left(Y_ZR, first(zrecv, NZ - 1))
    left(Y_XR, yct.at[:, pl.ds(0, (NX - 1) * QL)])
    left(P_ZR, first(zrecv, NZ - 1))
    left(S_RS, first(srecv, NG - 1))
    left(S_AG, first(sall, NZ - 1))

    @pl.when(own_quarter)
    def _():
        left(Y_B, first(zrecv, 15))

    @pl.when(jnp.logical_not(own_quarter))
    def _():
        left(Y_B, first(zrecv, 16))

    @pl.when(own_quarter)
    def _():
        left(P_SUB, first(zrecv, 15))

    @pl.when(jnp.logical_and(c == r // 2, jnp.logical_not(own_quarter)))
    def _():
        left(P_SUB, first(zrecv, 16))


def local(matrix, panel):
    vmem = pl.BlockSpec(memory_space=pltpu.VMEM)
    in_hbm = pl.BlockSpec(memory_space=pltpu.HBM)
    updated, weights = pl.pallas_call(
        panel_step,
        out_shape=(jax.ShapeDtypeStruct((RL, CL), F32), jax.ShapeDtypeStruct((B, RL), F32)),
        in_specs=[in_hbm, in_hbm],
        out_specs=(vmem, vmem),
        scratch_shapes=[
            pltpu.VMEM((B, RL), F32),
            pltpu.VMEM((B, CL), F32),
            pltpu.VMEM((NR, 8, QL), F32),
            pltpu.VMEM((NR, 2, 128), F32),
            pltpu.VMEM((NR, 2, 128), F32),
            pltpu.VMEM((1, 128), F32),
            pltpu.VMEM((NR, 1, 128), F32),
            pltpu.VMEM((B, CL), F32),
            pltpu.VMEM((B, 128), F32),
            pltpu.VMEM((8, QL), F32),
            pltpu.VMEM((B, CL), F32),
            pltpu.VMEM((B, RL), F32),
            pltpu.VMEM((4, 128), F32),
            pltpu.VMEM((NG, 4, 128), F32),
            pltpu.VMEM((4, 128), F32),
            pltpu.VMEM((NZ, 4, 128), F32),
            pltpu.SemaphoreType.DMA((2,)), pltpu.SemaphoreType.DMA((STAGES,)), pltpu.SemaphoreType.DMA((STAGES,)),
        ],
        compiler_params=pltpu.CompilerParams(
            collective_id=0, has_side_effects=True, vmem_limit_bytes=24 << 20),
        name="panel_step",
    )(pltpu.with_memory_space_constraint(matrix, pltpu.HBM), pltpu.with_memory_space_constraint(panel.T, pltpu.HBM))
    return updated, weights.T


def solution(mesh):
    specs = (P("row", "col"), P("row", None))
    return jax.shard_map(local, mesh=mesh, in_specs=specs, out_specs=specs, check_vma=False)
```

```python
import jax
import jax.numpy as jnp
from jax import lax
from jax.experimental import pallas as pl
from jax.experimental.pallas import tpu as pltpu
from jax.sharding import PartitionSpec as P

MESH = pl.DeviceIdType.MESH
F32 = jnp.float32
BF16 = jnp.bfloat16
NX, NZ, NC = 4, 8, 16
NR = NX * NZ
NG = NX * NC
B = 64
RL, CL = 512, 1024
QL = 256
TINY = 1e-30
G_RS, G_AG, P_SUB, P_ZR, P_XR, Z_RS, Y_ZR, Y_XR, Y_B, S_RS, S_AG = range(11)
STAGES = 11


def dot(a, b, dims=((1,), (0,))):
    return lax.dot_general(a, b, (dims, ((), ())), precision=lax.Precision.HIGHEST, preferred_element_type=F32)


def split(x):
    high = x.astype(BF16)
    return high, (x - high.astype(F32)).astype(BF16)


def split3(x):
    high = x.astype(BF16)
    rest = x - high.astype(F32)
    mid = rest.astype(BF16)
    return high, mid, (rest - mid.astype(F32)).astype(BF16)


def dot6(a, b):
    parts = jnp.concatenate(split3(a), axis=0)
    bh, bm, bl = split3(b)
    one = jnp.dot(parts, bh, preferred_element_type=F32)
    two = jnp.dot(parts[:2 * B], bm, preferred_element_type=F32)
    three = jnp.dot(parts[:B], bl, preferred_element_type=F32)
    return one[:B] + ((one[B:2 * B] + two[:B]) + (one[2 * B:] + two[B:] + three))


def dot3(at, b):
    ah, al = split(at.T)
    bh, bl = split(b)
    return jnp.dot(jnp.concatenate([ah, al, ah], axis=1), jnp.concatenate([bh, bh, bl], axis=0),
                   preferred_element_type=F32)


def inverse_factor(gram):
    row_id = lax.broadcasted_iota(jnp.int32, (B, 2 * B), 0)
    lane_id = lax.broadcasted_iota(jnp.int32, (B, 2 * B), 1)
    work = jnp.concatenate([gram, jnp.where(row_id == lane_id, 1.0, 0.0)[:, :B]], axis=1)
    step = 8
    for j in range(0, B, step):
        cols = [jnp.broadcast_to(work[:, j + t:j + t + 1], (B, 2 * B)) for t in range(step)]
        rows = [work[j + t:j + t + 1, :] for t in range(step)]
        for t in range(step):
            at = j + t
            ratio = jnp.where(row_id > at, cols[t] * (1.0 / cols[t][at:at + 1, :]), 0.0)
            work = work - ratio * rows[t]
            for u in range(t + 1, step):
                cols[u] = cols[u] - ratio * cols[t][j + u:j + u + 1, :]
                rows[u] = rows[u] - ratio[j + u:j + u + 1, :] * rows[t]
    pivots = jnp.sum(jnp.where(row_id == lane_id, work, 0.0), axis=1, keepdims=True)
    root = lax.rsqrt(pivots)
    root = root * (1.5 - 0.5 * pivots * root * root)
    return work[:, B:] * root


def panel_step(matrix_hbm, panel_hbm, out_ref, w_ref, basis_ref, turned_ref,
               pt, zt, zrecv, gsend, grecv, gown, gall, ct, spart,
               ypiece, yct, yrt, ssend, srecv, sown, sall, in_sem, send_sem, recv_sem):
    r = lax.axis_index("row")
    c = lax.axis_index("col")
    x, z = r // NZ, r % NZ
    feats = pl.ds(pl.multiple_of(z * 8, 8), 8)
    quarter = pl.ds(pl.multiple_of(x * QL, QL), QL)
    half = pl.ds(pl.multiple_of(lax.rem(x, 2) * QL, QL), QL)

    load_p = pltpu.make_async_copy(panel_hbm, pt, in_sem.at[0])
    load_a = pltpu.make_async_copy(matrix_hbm, out_ref, in_sem.at[1])
    load_p.start()
    load_a.start()

    def plane(i):
        return lax.rem(x + i // NZ, NX) * NZ + lax.rem(z + lax.rem(i, NZ), NZ)

    def line(i):
        return lax.rem(c + i, NC)

    barrier = pltpu.get_barrier_semaphore()

    def greet_plane(i, carry):
        pl.semaphore_signal(barrier, inc=1, device_id=(plane(i), c), device_id_type=MESH)
        return carry

    def greet_line(i, carry):
        pl.semaphore_signal(barrier, inc=1, device_id=(r, line(i)), device_id_type=MESH)
        return carry

    lax.fori_loop(1, NR, greet_plane, 0)
    lax.fori_loop(1, NC, greet_line, 0)

    def push(stage, src, dst, row, col):
        pltpu.make_async_remote_copy(
            src, dst, send_sem.at[stage], recv_sem.at[stage],
            device_id=(row, col), device_id_type=MESH).start()

    def to_plane(stage, src, dst):
        def send(i, carry):
            other = plane(i)
            push(stage, src(other), dst, other, c)
            return carry
        lax.fori_loop(1, NR, send, 0)

    def to_line(stage, src, dst):
        def send(i, carry):
            other = line(i)
            push(stage, src(other), dst, r, other)
            return carry
        lax.fori_loop(1, NC, send, 0)

    def arrived(stage, part):
        pltpu.make_async_copy(part, part, recv_sem.at[stage]).wait()

    def left(stage, part):
        pltpu.make_async_copy(part, part, send_sem.at[stage]).wait()

    def first(buf, n):
        return buf.at[pl.ds(0, n)]

    load_p.wait()
    own_scale = jnp.maximum(jnp.max(jnp.abs(pt[...]), axis=1, keepdims=True), TINY)
    gram = dot(pt[...], pt[...], ((1,), (1,)))
    gsend[:, 0, :] = jnp.concatenate([gram[:32], gram[32:]], axis=1)
    scale_row = jnp.broadcast_to(own_scale, (B, 128)).T[0:1, :]
    gsend[:, 1, :] = jnp.broadcast_to(jnp.concatenate([scale_row, scale_row], axis=1), (NR, 128))

    def multiply():
        load_a.wait()
        zt[...] = dot6(pt[...] * (1.0 / (128.0 * own_scale)), out_ref[...])

    @pl.when(z < NZ // 2)
    def _():
        multiply()

    pl.semaphore_wait(barrier, NR - 1 + NC - 1)
    def spread_quarters(i, carry):
        ox = 2 * lax.rem(r, 2) + i // NZ
        oz = lax.rem(z + lax.rem(i, NZ), NZ)
        other = ox * NZ + oz

        @pl.when(other != r)
        def _():
            push(P_SUB, pt.at[pl.ds(pl.multiple_of(oz * 8, 8), 8), pl.ds(pl.multiple_of((i // NZ) * QL, QL), QL)],
                 ct.at[pl.ds(pl.multiple_of(oz * 8, 8), 8), pl.ds(pl.multiple_of(ox * QL, QL), QL)], other, c)
        return carry

    @pl.when(c == r // 2)
    def _():
        lax.fori_loop(0, 2 * NZ, spread_quarters, 0)

    own_quarter = r == 2 * c + x // 2

    @pl.when(own_quarter)
    def _():
        ct[feats, quarter] = pt[feats, half]

    to_plane(G_RS, lambda o: gsend.at[o], grecv.at[r])
    grecv[r] = gsend[r]

    @pl.when(z >= NZ // 2)
    def _():
        multiply()

    def send_pieces(i, carry):
        other = plane(i)
        push(Z_RS, zt.at[pl.ds(pl.multiple_of(lax.rem(other, NZ) * 8, 8), 8),
                         pl.ds(pl.multiple_of((other // NZ) * QL, QL), QL)], zrecv.at[r], other, c)
        return carry
    lax.fori_loop(1, NR, send_pieces, 0)
    zrecv[r] = zt[feats, quarter]

    @pl.when(jnp.logical_not(own_quarter))
    def _():
        arrived(P_SUB, ct.at[feats, quarter])

    def hand_round(i, carry):
        push(P_ZR, ct.at[feats, quarter], ct.at[feats, quarter], x * NZ + lax.rem(z + i, NZ), c)
        return carry
    lax.fori_loop(1, NZ, hand_round, 0)

    arrived(G_RS, first(grecv, NR - 1))
    gown[...] = jnp.sum(grecv[:, 0, :], axis=0, keepdims=True)
    to_plane(G_AG, lambda o: gown, gall.at[r])
    gall[r] = gown[...]
    scales = jnp.broadcast_to(grecv[:, 1, :][None], (4, NR, 128)).reshape(4 * NR, 128).T[:B]
    scale = jnp.max(scales, axis=1, keepdims=True)
    inv_scale = 1.0 / (128.0 * scale)
    spart[...] = scales * (1.0 / scale)
    share = spart[feats, :]

    arrived(Z_RS, first(zrecv, NR - 1))
    total = zrecv[0] * share[:, 0:1]
    for k in range(1, NR):
        total = total + zrecv[k] * share[:, k:k + 1]
    ypiece[...] = total
    def hand_product(i, carry):
        push(Y_ZR, ypiece, yct.at[feats, quarter], x * NZ + lax.rem(z + i, NZ), c)
        return carry
    lax.fori_loop(1, NZ, hand_product, 0)
    yct[feats, quarter] = total

    arrived(P_ZR, first(zrecv, NZ - 1))
    part = dot(total, ct[:, quarter] * inv_scale, ((1,), (1,)))
    ssend[...] = jnp.concatenate([part[:4], part[4:]], axis=1)

    def send_coupling(i, carry):
        push(S_RS, ssend, srecv.at[x * NC + c],
             lax.rem(x + i // NC, NX) * NZ + z, lax.rem(c + lax.rem(i, NC), NC))
        return carry
    lax.fori_loop(1, NG, send_coupling, 0)
    srecv[x * NC + c] = ssend[...]

    def send_rows(i, carry):
        block = 2 * c + x // 2
        other = line(i)

        @pl.when(jnp.logical_or(block != r, other != c))
        def _():
            push(Y_B, ypiece, yrt.at[feats, half], block, other)
        return carry
    lax.fori_loop(0, NC, send_rows, 0)

    @pl.when(own_quarter)
    def _():
        yrt[feats, half] = total

    def hand_across(i, carry):
        push(P_XR, ct.at[:, quarter], ct.at[:, quarter], lax.rem(x + i, NX) * NZ + z, c)
        return carry
    lax.fori_loop(1, NX, hand_across, 0)

    arrived(G_AG, first(gall, NR - 1))
    g32 = gall[:, 0, :]
    gram = jnp.concatenate([g32[:, :B], g32[:, B:]], axis=0)
    inv_row = jnp.broadcast_to(inv_scale, (B, 128)).T[0:1, :]
    inv_lower = inverse_factor(gram * inv_scale * inv_row)
    unscaled = inv_lower * inv_row
    arrived(Y_ZR, first(zrecv, NZ - 1))

    def hand_product_across(i, carry):
        push(Y_XR, yct.at[:, quarter], yct.at[:, quarter], lax.rem(x + i, NX) * NZ + z, c)
        return carry
    lax.fori_loop(1, NX, hand_product_across, 0)

    basis_r = dot(unscaled, pt[...])

    arrived(S_RS, first(srecv, NG - 1))
    sown[...] = jnp.sum(srecv[...], axis=0)

    def send_rows_of_coupling(i, carry):
        push(S_AG, sown, sall.at[z], x * NZ + lax.rem(z + i, NZ), c)
        return carry
    lax.fori_loop(1, NZ, send_rows_of_coupling, 0)
    sall[z] = sown[...]

    arrived(Y_XR, yct.at[:, pl.ds(0, (NX - 1) * QL)])
    product_c = dot(inv_lower, yct[...])

    arrived(P_XR, ct.at[:, pl.ds(0, (NX - 1) * QL)])
    basis_c = dot(unscaled, ct[...])

    @pl.when(own_quarter)
    def _():
        arrived(Y_B, first(zrecv, 15))

    @pl.when(jnp.logical_not(own_quarter))
    def _():
        arrived(Y_B, first(zrecv, 16))
    product_r = dot(inv_lower, yrt[...])

    tile = 128
    for t in range(RL // tile):
        cols = pl.ds(t * tile, tile)
        ours = jnp.concatenate([basis_r[:, t * tile:(t + 1) * tile], product_r[:, t * tile:(t + 1) * tile]], axis=0)
        out_ref[cols, :] -= dot3(2.0 * ours, jnp.concatenate([product_c, basis_c], axis=0))

    arrived(S_AG, first(sall, NZ - 1))
    inner = jnp.concatenate([sall[k][:, h * B:(h + 1) * B] for k in range(NZ) for h in range(2)], axis=0)
    coupling = dot(dot(inv_lower, inner), inv_lower, ((1,), (1,)))
    w_ref[...] = 2.0 * product_r - 2.0 * dot(coupling, basis_r)
    turned_ref[...] = 4.0 * dot(coupling, basis_c)
    basis_ref[...] = basis_r

    left(G_RS, first(gsend, NR - 1))
    left(G_AG, first(gall, NR - 1))
    left(Z_RS, first(zrecv, NR - 1))
    left(P_XR, ct.at[:, pl.ds(0, (NX - 1) * QL)])
    left(Y_ZR, first(zrecv, NZ - 1))
    left(Y_XR, yct.at[:, pl.ds(0, (NX - 1) * QL)])
    left(P_ZR, first(zrecv, NZ - 1))
    left(S_RS, first(srecv, NG - 1))
    left(S_AG, first(sall, NZ - 1))

    @pl.when(own_quarter)
    def _():
        left(Y_B, first(zrecv, 15))

    @pl.when(jnp.logical_not(own_quarter))
    def _():
        left(Y_B, first(zrecv, 16))

    @pl.when(own_quarter)
    def _():
        left(P_SUB, first(zrecv, 15))

    @pl.when(jnp.logical_and(c == r // 2, jnp.logical_not(own_quarter)))
    def _():
        left(P_SUB, first(zrecv, 16))


def finish(part_ref, w_ref, basis_ref, turned_ref, out_hbm, w_hbm, out_v, sem, w_sem):
    w_copy = pltpu.make_async_copy(w_ref, w_hbm, w_sem)
    w_copy.start()
    tile = 128
    copies = []
    for t in range(RL // tile):
        rows = pl.ds(t * tile, tile)
        out_v[rows, :] = part_ref[rows, :] + dot3(basis_ref[:, t * tile:(t + 1) * tile], turned_ref[...])
        copies.append(pltpu.make_async_copy(out_v.at[rows], out_hbm.at[rows], sem.at[t]))
        copies[-1].start()
    for copy in copies:
        copy.wait()
    w_copy.wait()


def local(matrix, panel):
    vmem = pl.BlockSpec(memory_space=pltpu.VMEM)
    in_hbm = pl.BlockSpec(memory_space=pltpu.HBM)
    part, weights, basis, turned = pl.pallas_call(
        panel_step,
        out_shape=(jax.ShapeDtypeStruct((RL, CL), F32), jax.ShapeDtypeStruct((B, RL), F32),
                   jax.ShapeDtypeStruct((B, RL), F32), jax.ShapeDtypeStruct((B, CL), F32)),
        in_specs=[in_hbm, in_hbm],
        out_specs=(vmem, vmem, vmem, vmem),
        scratch_shapes=[
            pltpu.VMEM((B, RL), F32),
            pltpu.VMEM((B, CL), F32),
            pltpu.VMEM((NR, 8, QL), F32),
            pltpu.VMEM((NR, 2, 128), F32),
            pltpu.VMEM((NR, 2, 128), F32),
            pltpu.VMEM((1, 128), F32),
            pltpu.VMEM((NR, 1, 128), F32),
            pltpu.VMEM((B, CL), F32),
            pltpu.VMEM((B, 128), F32),
            pltpu.VMEM((8, QL), F32),
            pltpu.VMEM((B, CL), F32),
            pltpu.VMEM((B, RL), F32),
            pltpu.VMEM((4, 128), F32),
            pltpu.VMEM((NG, 4, 128), F32),
            pltpu.VMEM((4, 128), F32),
            pltpu.VMEM((NZ, 4, 128), F32),
            pltpu.SemaphoreType.DMA((2,)), pltpu.SemaphoreType.DMA((STAGES,)), pltpu.SemaphoreType.DMA((STAGES,)),
        ],
        compiler_params=pltpu.CompilerParams(
            collective_id=0, has_side_effects=True, vmem_limit_bytes=24 << 20),
        name="panel_step",
    )(pltpu.with_memory_space_constraint(matrix, pltpu.HBM), pltpu.with_memory_space_constraint(panel.T, pltpu.HBM))
    updated, weights = pl.pallas_call(
        finish,
        out_shape=(jax.ShapeDtypeStruct((RL, CL), F32), jax.ShapeDtypeStruct((B, RL), F32)),
        in_specs=[vmem, vmem, vmem, vmem],
        out_specs=(in_hbm, in_hbm),
        scratch_shapes=[pltpu.VMEM((RL, CL), F32), pltpu.SemaphoreType.DMA((4,)), pltpu.SemaphoreType.DMA],
        compiler_params=pltpu.CompilerParams(vmem_limit_bytes=24 << 20),
        name="finish",
    )(part, weights, basis, turned)
    return updated, weights.T


def solution(mesh):
    specs = (P("row", "col"), P("row", None))
    return jax.shard_map(local, mesh=mesh, in_specs=specs, out_specs=specs, check_vma=False)
```

```python
import jax
import jax.numpy as jnp
from jax import lax
from jax.experimental import pallas as pl
from jax.experimental.pallas import tpu as pltpu
from jax.sharding import PartitionSpec as P

MESH = pl.DeviceIdType.MESH
F32 = jnp.float32
BF16 = jnp.bfloat16
NX, NZ, NC = 4, 8, 16
NR = NX * NZ
NG = NX * NC
B = 64
RL, CL = 512, 1024
QL = 256
TINY = 1e-30
G_RS, G_AG, P_SUB, P_ZR, P_XR, Z_RS, Y_ZR, Y_XR, Y_B, S_RS, S_AG = range(11)
STAGES = 11


def dot(a, b, dims=((1,), (0,))):
    return lax.dot_general(a, b, (dims, ((), ())), precision=lax.Precision.HIGHEST, preferred_element_type=F32)


def split(x):
    high = x.astype(BF16)
    return high, (x - high.astype(F32)).astype(BF16)


def split3(x):
    high = x.astype(BF16)
    rest = x - high.astype(F32)
    mid = rest.astype(BF16)
    return high, mid, (rest - mid.astype(F32)).astype(BF16)


def dot6(a, b):
    parts = jnp.concatenate(split3(a), axis=0)
    bh, bm, bl = split3(b)
    one = jnp.dot(parts, bh, preferred_element_type=F32)
    two = jnp.dot(parts[:2 * B], bm, preferred_element_type=F32)
    three = jnp.dot(parts[:B], bl, preferred_element_type=F32)
    return one[:B] + ((one[B:2 * B] + two[:B]) + (one[2 * B:] + two[B:] + three))


def dot3(at, b):
    ah, al = split(at.T)
    bh, bl = split(b)
    return jnp.dot(jnp.concatenate([ah, al, ah], axis=1), jnp.concatenate([bh, bh, bl], axis=0),
                   preferred_element_type=F32)


def inverse_factor(gram):
    row_id = lax.broadcasted_iota(jnp.int32, (B, 2 * B), 0)
    lane_id = lax.broadcasted_iota(jnp.int32, (B, 2 * B), 1)
    work = jnp.concatenate([gram, jnp.where(row_id == lane_id, 1.0, 0.0)[:, :B]], axis=1)
    step = 8
    for j in range(0, B, step):
        cols = [jnp.broadcast_to(work[:, j + t:j + t + 1], (B, 2 * B)) for t in range(step)]
        rows = [work[j + t:j + t + 1, :] for t in range(step)]
        for t in range(step):
            at = j + t
            ratio = jnp.where(row_id > at, cols[t] * (1.0 / cols[t][at:at + 1, :]), 0.0)
            work = work - ratio * rows[t]
            for u in range(t + 1, step):
                cols[u] = cols[u] - ratio * cols[t][j + u:j + u + 1, :]
                rows[u] = rows[u] - ratio[j + u:j + u + 1, :] * rows[t]
    pivots = jnp.sum(jnp.where(row_id == lane_id, work, 0.0), axis=1, keepdims=True)
    root = lax.rsqrt(pivots)
    root = root * (1.5 - 0.5 * pivots * root * root)
    return work[:, B:] * root


def panel_step(matrix_hbm, panel_hbm, out_ref, w_ref, basis_ref, turned_ref,
               pt, zt, zrecv, gsend, grecv, gown, gall, ct, spart,
               ypiece, yct, yrt, ssend, srecv, sown, sall, in_sem, send_sem, recv_sem):
    r = lax.axis_index("row")
    c = lax.axis_index("col")
    x, z = r // NZ, r % NZ
    feats = pl.ds(pl.multiple_of(z * 8, 8), 8)
    quarter = pl.ds(pl.multiple_of(x * QL, QL), QL)
    half = pl.ds(pl.multiple_of(lax.rem(x, 2) * QL, QL), QL)

    load_p = pltpu.make_async_copy(panel_hbm, pt, in_sem.at[0])
    load_a = pltpu.make_async_copy(matrix_hbm, out_ref, in_sem.at[1])
    load_p.start()
    load_a.start()

    def plane(i):
        return lax.rem(x + i // NZ, NX) * NZ + lax.rem(z + lax.rem(i, NZ), NZ)

    def line(i):
        return lax.rem(c + i, NC)

    barrier = pltpu.get_barrier_semaphore()

    def greet_plane(i, carry):
        pl.semaphore_signal(barrier, inc=1, device_id=(plane(i), c), device_id_type=MESH)
        return carry

    def greet_line(i, carry):
        pl.semaphore_signal(barrier, inc=1, device_id=(r, line(i)), device_id_type=MESH)
        return carry

    lax.fori_loop(1, NR, greet_plane, 0)
    lax.fori_loop(1, NC, greet_line, 0)

    def push(stage, src, dst, row, col):
        pltpu.make_async_remote_copy(
            src, dst, send_sem.at[stage], recv_sem.at[stage],
            device_id=(row, col), device_id_type=MESH).start()

    def to_plane(stage, src, dst):
        def send(i, carry):
            other = plane(i)
            push(stage, src(other), dst, other, c)
            return carry
        lax.fori_loop(1, NR, send, 0)

    def to_line(stage, src, dst):
        def send(i, carry):
            other = line(i)
            push(stage, src(other), dst, r, other)
            return carry
        lax.fori_loop(1, NC, send, 0)

    def arrived(stage, part):
        pltpu.make_async_copy(part, part, recv_sem.at[stage]).wait()

    def left(stage, part):
        pltpu.make_async_copy(part, part, send_sem.at[stage]).wait()

    def first(buf, n):
        return buf.at[pl.ds(0, n)]

    load_p.wait()
    own_scale = jnp.maximum(jnp.max(jnp.abs(pt[...]), axis=1, keepdims=True), TINY)
    gram = dot(pt[...], pt[...], ((1,), (1,)))
    gsend[:, 0, :] = jnp.concatenate([gram[:32], gram[32:]], axis=1)
    scale_row = jnp.broadcast_to(own_scale, (B, 128)).T[0:1, :]
    gsend[:, 1, :] = jnp.broadcast_to(jnp.concatenate([scale_row, scale_row], axis=1), (NR, 128))

    def multiply():
        load_a.wait()
        zt[...] = dot6(pt[...] * (1.0 / (128.0 * own_scale)), out_ref[...])

    @pl.when(z < NZ // 2)
    def _():
        multiply()

    pl.semaphore_wait(barrier, NR - 1 + NC - 1)
    def spread_quarters(i, carry):
        ox = 2 * lax.rem(r, 2) + i // NZ
        oz = lax.rem(z + lax.rem(i, NZ), NZ)
        other = ox * NZ + oz

        @pl.when(other != r)
        def _():
            push(P_SUB, pt.at[pl.ds(pl.multiple_of(oz * 8, 8), 8), pl.ds(pl.multiple_of((i // NZ) * QL, QL), QL)],
                 ct.at[pl.ds(pl.multiple_of(oz * 8, 8), 8), pl.ds(pl.multiple_of(ox * QL, QL), QL)], other, c)
        return carry

    @pl.when(c == r // 2)
    def _():
        lax.fori_loop(0, 2 * NZ, spread_quarters, 0)

    own_quarter = r == 2 * c + x // 2

    @pl.when(own_quarter)
    def _():
        ct[feats, quarter] = pt[feats, half]

    to_plane(G_RS, lambda o: gsend.at[o], grecv.at[r])
    grecv[r] = gsend[r]

    @pl.when(z >= NZ // 2)
    def _():
        multiply()

    def send_pieces(i, carry):
        other = plane(i)
        push(Z_RS, zt.at[pl.ds(pl.multiple_of(lax.rem(other, NZ) * 8, 8), 8),
                         pl.ds(pl.multiple_of((other // NZ) * QL, QL), QL)], zrecv.at[r], other, c)
        return carry
    lax.fori_loop(1, NR, send_pieces, 0)
    zrecv[r] = zt[feats, quarter]

    @pl.when(jnp.logical_not(own_quarter))
    def _():
        arrived(P_SUB, ct.at[feats, quarter])

    def hand_round(i, carry):
        push(P_ZR, ct.at[feats, quarter], ct.at[feats, quarter], x * NZ + lax.rem(z + i, NZ), c)
        return carry
    lax.fori_loop(1, NZ, hand_round, 0)

    arrived(G_RS, first(grecv, NR - 1))
    gown[...] = jnp.sum(grecv[:, 0, :], axis=0, keepdims=True)
    to_plane(G_AG, lambda o: gown, gall.at[r])
    gall[r] = gown[...]
    scales = jnp.broadcast_to(grecv[:, 1, :][None], (4, NR, 128)).reshape(4 * NR, 128).T[:B]
    scale = jnp.max(scales, axis=1, keepdims=True)
    inv_scale = 1.0 / (128.0 * scale)
    spart[...] = scales * (1.0 / scale)
    share = spart[feats, :]

    arrived(Z_RS, first(zrecv, NR - 1))
    total = zrecv[0] * share[:, 0:1]
    for k in range(1, NR):
        total = total + zrecv[k] * share[:, k:k + 1]
    ypiece[...] = total
    def hand_product(i, carry):
        push(Y_ZR, ypiece, yct.at[feats, quarter], x * NZ + lax.rem(z + i, NZ), c)
        return carry
    lax.fori_loop(1, NZ, hand_product, 0)
    yct[feats, quarter] = total

    arrived(P_ZR, first(zrecv, NZ - 1))
    part = dot(total, ct[:, quarter] * inv_scale, ((1,), (1,)))
    ssend[...] = jnp.concatenate([part[:4], part[4:]], axis=1)

    def send_coupling(i, carry):
        push(S_RS, ssend, srecv.at[x * NC + c],
             lax.rem(x + i // NC, NX) * NZ + z, lax.rem(c + lax.rem(i, NC), NC))
        return carry
    lax.fori_loop(1, NG, send_coupling, 0)
    srecv[x * NC + c] = ssend[...]

    def send_rows(i, carry):
        block = 2 * c + x // 2
        other = line(i)

        @pl.when(jnp.logical_or(block != r, other != c))
        def _():
            push(Y_B, ypiece, yrt.at[feats, half], block, other)
        return carry
    lax.fori_loop(0, NC, send_rows, 0)

    @pl.when(own_quarter)
    def _():
        yrt[feats, half] = total

    def hand_across(i, carry):
        push(P_XR, ct.at[:, quarter], ct.at[:, quarter], lax.rem(x + 1 + lax.rem(i, 3), NX) * NZ + z, c)
        return carry
    lax.fori_loop(1, NX, hand_across, 0)

    arrived(G_AG, first(gall, NR - 1))
    g32 = gall[:, 0, :]
    gram = jnp.concatenate([g32[:, :B], g32[:, B:]], axis=0)
    inv_row = jnp.broadcast_to(inv_scale, (B, 128)).T[0:1, :]
    inv_lower = inverse_factor(gram * inv_scale * inv_row)
    unscaled = inv_lower * inv_row
    arrived(Y_ZR, first(zrecv, NZ - 1))

    def hand_product_across(i, carry):
        push(Y_XR, yct.at[:, quarter], yct.at[:, quarter], lax.rem(x + 1 + lax.rem(i, 3), NX) * NZ + z, c)
        return carry
    lax.fori_loop(1, NX, hand_product_across, 0)

    basis_r = dot(unscaled, pt[...])

    arrived(S_RS, first(srecv, NG - 1))
    sown[...] = jnp.sum(srecv[...], axis=0)

    def send_rows_of_coupling(i, carry):
        push(S_AG, sown, sall.at[z], x * NZ + lax.rem(z + i, NZ), c)
        return carry
    lax.fori_loop(1, NZ, send_rows_of_coupling, 0)
    sall[z] = sown[...]

    arrived(Y_XR, yct.at[:, pl.ds(0, (NX - 1) * QL)])
    product_c = dot(inv_lower, yct[...])

    arrived(P_XR, ct.at[:, pl.ds(0, (NX - 1) * QL)])
    basis_c = dot(unscaled, ct[...])

    @pl.when(own_quarter)
    def _():
        arrived(Y_B, first(zrecv, 15))

    @pl.when(jnp.logical_not(own_quarter))
    def _():
        arrived(Y_B, first(zrecv, 16))
    product_r = dot(inv_lower, yrt[...])

    tile = 128
    for t in range(RL // tile):
        cols = pl.ds(t * tile, tile)
        ours = jnp.concatenate([basis_r[:, t * tile:(t + 1) * tile], product_r[:, t * tile:(t + 1) * tile]], axis=0)
        out_ref[cols, :] -= dot3(2.0 * ours, jnp.concatenate([product_c, basis_c], axis=0))

    arrived(S_AG, first(sall, NZ - 1))
    inner = jnp.concatenate([sall[k][:, h * B:(h + 1) * B] for k in range(NZ) for h in range(2)], axis=0)
    coupling = dot(dot(inv_lower, inner), inv_lower, ((1,), (1,)))
    w_ref[...] = 2.0 * product_r - 2.0 * dot(coupling, basis_r)
    turned_ref[...] = 4.0 * dot(coupling, basis_c)
    basis_ref[...] = basis_r

    left(G_RS, first(gsend, NR - 1))
    left(G_AG, first(gall, NR - 1))
    left(Z_RS, first(zrecv, NR - 1))
    left(P_XR, ct.at[:, pl.ds(0, (NX - 1) * QL)])
    left(Y_ZR, first(zrecv, NZ - 1))
    left(Y_XR, yct.at[:, pl.ds(0, (NX - 1) * QL)])
    left(P_ZR, first(zrecv, NZ - 1))
    left(S_RS, first(srecv, NG - 1))
    left(S_AG, first(sall, NZ - 1))

    @pl.when(own_quarter)
    def _():
        left(Y_B, first(zrecv, 15))

    @pl.when(jnp.logical_not(own_quarter))
    def _():
        left(Y_B, first(zrecv, 16))

    @pl.when(own_quarter)
    def _():
        left(P_SUB, first(zrecv, 15))

    @pl.when(jnp.logical_and(c == r // 2, jnp.logical_not(own_quarter)))
    def _():
        left(P_SUB, first(zrecv, 16))


def finish(part_ref, w_ref, basis_ref, turned_ref, out_hbm, w_hbm, out_v, sem, w_sem):
    w_copy = pltpu.make_async_copy(w_ref, w_hbm, w_sem)
    w_copy.start()
    tile = 128
    copies = []
    for t in range(RL // tile):
        rows = pl.ds(t * tile, tile)
        out_v[rows, :] = part_ref[rows, :] + dot3(basis_ref[:, t * tile:(t + 1) * tile], turned_ref[...])
        copies.append(pltpu.make_async_copy(out_v.at[rows], out_hbm.at[rows], sem.at[t]))
        copies[-1].start()
    for copy in copies:
        copy.wait()
    w_copy.wait()


def local(matrix, panel):
    vmem = pl.BlockSpec(memory_space=pltpu.VMEM)
    in_hbm = pl.BlockSpec(memory_space=pltpu.HBM)
    part, weights, basis, turned = pl.pallas_call(
        panel_step,
        out_shape=(jax.ShapeDtypeStruct((RL, CL), F32), jax.ShapeDtypeStruct((B, RL), F32),
                   jax.ShapeDtypeStruct((B, RL), F32), jax.ShapeDtypeStruct((B, CL), F32)),
        in_specs=[in_hbm, in_hbm],
        out_specs=(vmem, vmem, vmem, vmem),
        scratch_shapes=[
            pltpu.VMEM((B, RL), F32),
            pltpu.VMEM((B, CL), F32),
            pltpu.VMEM((NR, 8, QL), F32),
            pltpu.VMEM((NR, 2, 128), F32),
            pltpu.VMEM((NR, 2, 128), F32),
            pltpu.VMEM((1, 128), F32),
            pltpu.VMEM((NR, 1, 128), F32),
            pltpu.VMEM((B, CL), F32),
            pltpu.VMEM((B, 128), F32),
            pltpu.VMEM((8, QL), F32),
            pltpu.VMEM((B, CL), F32),
            pltpu.VMEM((B, RL), F32),
            pltpu.VMEM((4, 128), F32),
            pltpu.VMEM((NG, 4, 128), F32),
            pltpu.VMEM((4, 128), F32),
            pltpu.VMEM((NZ, 4, 128), F32),
            pltpu.SemaphoreType.DMA((2,)), pltpu.SemaphoreType.DMA((STAGES,)), pltpu.SemaphoreType.DMA((STAGES,)),
        ],
        compiler_params=pltpu.CompilerParams(
            collective_id=0, has_side_effects=True, vmem_limit_bytes=24 << 20),
        name="panel_step",
    )(pltpu.with_memory_space_constraint(matrix, pltpu.HBM), pltpu.with_memory_space_constraint(panel.T, pltpu.HBM))
    updated, weights = pl.pallas_call(
        finish,
        out_shape=(jax.ShapeDtypeStruct((RL, CL), F32), jax.ShapeDtypeStruct((B, RL), F32)),
        in_specs=[vmem, vmem, vmem, vmem],
        out_specs=(in_hbm, in_hbm),
        scratch_shapes=[pltpu.VMEM((RL, CL), F32), pltpu.SemaphoreType.DMA((4,)), pltpu.SemaphoreType.DMA],
        compiler_params=pltpu.CompilerParams(vmem_limit_bytes=24 << 20),
        name="finish",
    )(part, weights, basis, turned)
    return updated, weights.T


def solution(mesh):
    specs = (P("row", "col"), P("row", None))
    return jax.shard_map(local, mesh=mesh, in_specs=specs, out_specs=specs, check_vma=False)
```
